32 devices in a mesh: leaf: 32 (over z, y, x, core).
Axes of the slice: x: 2, y: 2, z: 4, core: 2. Of those that a mesh axis runs over, the one named last changes fastest.
Arguments:
- white_noise: float32 [32768, 128], P('leaf'), may hold values from -6 to 6
- leaf_inverse: float32 [32768, 1024], P('leaf'), may hold values from -1 to 4, as said below
- bases: float32 [32768, 640], P('leaf'), may hold values from -2 to 2
Outputs:
- solution: float32 [32768, 128], P('leaf')
The draws below stay inside these ranges and needn't reach their ends.
Inputs may be any that keep to these rules, and one draw needn't show every extreme that they name: `leaf_inverse`: each leaf's block of 1024 rows is symmetric positive definite.
All inputs are finite; a program needn't handle non-finite values.
Results may differ from the reference program's by a relative error of at most 0.0001.
Values sent between devices are 32-bit elements; how exact they have to be, the bound alone decides.
A program may use at most 128 MiB of HBM per device.

```python
import math
import jax
import jax.numpy as jnp
from jax import lax

LEAF = 1024
R = 128
SAMPLES = 128
LEVELS = 5
NCELLS = 32768
N_LEAF = 32


def draw_leaf_inverse(key, part):
    key_diag = jax.random.fold_in(key, 11)
    key_sym = jax.random.fold_in(key, 12)
    raw = jnp.clip(jax.random.normal(key_sym, (N_LEAF, LEAF, LEAF), jnp.float32), -4.0, 4.0)
    diagonal = jax.random.uniform(key_diag, (N_LEAF, LEAF), jnp.float32, minval=1.0, maxval=2.0)
    symmetric = (raw + jnp.swapaxes(raw, 1, 2)) * (0.25 / math.sqrt(LEAF))
    matrix = symmetric + diagonal[:, :, None] * jnp.eye(LEAF, dtype=jnp.float32)[None, :, :]
    return matrix.reshape(N_LEAF * LEAF, LEAF)


def draw_bases(key, part):
    key_main = jax.random.fold_in(key, 21)
    scales = 2.0 / jnp.sqrt(LEAF * 2.0 ** (jnp.arange(LEVELS).astype(jnp.float32) + 1.0))
    raw = jnp.clip(jax.random.normal(key_main, (N_LEAF * LEAF, LEVELS, R), jnp.float32), -4.0, 4.0)
    return (raw * scales[None, :, None]).reshape(N_LEAF * LEAF, LEVELS * R)


def shard_levels(rng, extent, split, least, top_value):
    def one(dim, shards_of):
        steps = jax.random.uniform(jax.random.fold_in(jax.random.fold_in(rng, 6), dim), (shards_of,), jnp.float32, least / len(split), top_value / len(split))
        return jnp.repeat(jnp.exp(steps), extent[dim] // shards_of).reshape((-1,) + (1,) * (len(extent) - dim - 1))

    factor_of = one(*split[0])
    for cut in split[1:]:
        factor_of = factor_of * one(*cut)
    return factor_of


def scatter_about(stream_key, extent, deviation, limit, shards=(), held_as=jnp.bfloat16):
    level = shard_levels(stream_key, extent, shards, -0.22, 0.18) if shards else 1.0
    result = jax.random.normal(stream_key, extent, jnp.float32) * deviation * level
    return jnp.minimum(jnp.maximum(result, -limit), limit).astype(held_as)


def setup_inputs(seed: int = 0) -> dict:
    splits = jax.random.split(jax.random.key(seed), 4)
    white_noise = scatter_about(splits[0], (NCELLS, SAMPLES), 1.0, 6.0, ((0, 32),), jnp.float32)
    leaf_inverse = draw_leaf_inverse(jax.random.fold_in(splits[3], 71), 0)
    bases = draw_bases(jax.random.fold_in(splits[3], 71), 0)
    return dict(white_noise=white_noise, leaf_inverse=leaf_inverse, bases=bases)


def reference(white_noise, leaf_inverse, bases):
    matrices = leaf_inverse.reshape(N_LEAF, LEAF, LEAF)
    combined = jnp.concatenate([bases, white_noise], axis=1).reshape(N_LEAF, LEAF, LEVELS * R + SAMPLES)
    solved = jnp.einsum('nij,njc->nic', matrices, combined, precision=lax.Precision.HIGHEST)
    basis_all = bases.reshape(N_LEAF, LEAF, LEVELS * R)
    for tree_level in range(LEVELS):
        width_leaves = 2 ** (tree_level + 1)
        level_basis = basis_all[:, :, tree_level * R:(tree_level + 1) * R]
        products = jnp.einsum('nkr,nkc->nrc', level_basis, solved, precision=lax.Precision.HIGHEST)
        group_sums = products.reshape(N_LEAF // width_leaves, width_leaves, R, -1).sum(axis=1)
        capacity = jnp.eye(R, dtype=jnp.float32) + group_sums[:, :, :R]
        factor = jnp.linalg.cholesky(capacity)
        forward = jax.scipy.linalg.solve_triangular(factor, group_sums[:, :, R:], lower=True)
        weights = jax.scipy.linalg.solve_triangular(factor, forward, lower=True, trans=1)
        spread = jnp.repeat(weights, width_leaves, axis=0)
        solved = solved[:, :, R:] - jnp.einsum('nkr,nrc->nkc', solved[:, :, :R], spread, precision=lax.Precision.HIGHEST)
    return solved.reshape(N_LEAF * LEAF, SAMPLES)
```

```python
import functools

import jax
import jax.numpy as jnp
from jax import lax
from jax.experimental import pallas as pl
from jax.experimental.pallas import tpu as pltpu
from jax.sharding import PartitionSpec as P

R = 128
PANEL = 16
F32 = jnp.float32
BF16 = jnp.bfloat16


def split2(x):
    high = x.astype(BF16)
    return high, (x - high.astype(F32)).astype(BF16)


def split3(x):
    high = x.astype(BF16)
    rest = x - high.astype(F32)
    mid = rest.astype(BF16)
    return high, mid, (rest - mid.astype(F32)).astype(BF16)


def mxu(a, b, dim):
    return lax.dot_general(a, b, (((dim,), (0,)), ((), ())), preferred_element_type=F32)


def product(a, b, dim=1):
    a_high, a_low = split2(a)
    b_high, b_low = split2(b)
    return mxu(a_high, b_high, dim) + (mxu(a_high, b_low, dim) + mxu(a_low, b_high, dim))


def negative_inverse(work):
    size = work.shape[0]
    row = lax.broadcasted_iota(jnp.int32, (PANEL, size), 0)
    lane = lax.broadcasted_iota(jnp.int32, (PANEL, size), 1)
    whole_row = lax.broadcasted_iota(jnp.int32, (size, size), 0)
    whole_lane = lax.broadcasted_iota(jnp.int32, (size, size), 1)

    def step(block, carry):
        base = pl.multiple_of(block * PANEL, PANEL)
        panel = work[pl.ds(base, PANEL), :]
        columns = [
            jnp.broadcast_to(
                jnp.sum(jnp.where(lane == base + j, panel, 0.0), axis=1, keepdims=True), (PANEL, size)
            )
            for j in range(PANEL)
        ]
        inside = (lane >= base) & (lane < base + PANEL)
        bordered = jnp.where(inside, jnp.where(lane == base + row, -1.0, 0.0), panel)
        reduced = bordered
        scale = jnp.ones((PANEL, size), F32)
        for k in range(PANEL):
            pivot = 1.0 / jnp.broadcast_to(columns[k][k : k + 1], (PANEL, size))
            factor = jnp.where(row == k, 0.0, columns[k] * pivot)
            scale = jnp.where(row == k, pivot, scale)
            for j in range(k + 1, PANEL):
                columns[j] = columns[j] - factor * jnp.broadcast_to(columns[j][k : k + 1], (PANEL, size))
            reduced = reduced - factor * jnp.broadcast_to(reduced[k : k + 1], (PANEL, size))
        a1, a2, a3 = split3(bordered)
        b1, b2, b3 = split3(reduced * scale)
        update = mxu(
            jnp.concatenate([a1, a1, a2, a1, a3, a2], axis=0),
            jnp.concatenate([b1, b2, b1, b3, b1, b2], axis=0),
            0,
        )
        crossed = (whole_row >= base) & (whole_row < base + PANEL)
        crossed |= (whole_lane >= base) & (whole_lane < base + PANEL)
        work[...] = jnp.where(crossed, 0.0, work[...]) - update
        return carry

    lax.fori_loop(0, size // PANEL, step, 0)


def tree_kernel(levels, gram, coefficients, *scratch):
    mine = [gram] + list(scratch[: levels - 1])
    theirs = scratch[levels - 1 : 2 * levels - 1]
    weights = scratch[2 * levels - 1 : 3 * levels - 1]
    work, send_sem, recv_sem = scratch[3 * levels - 1 :]
    me = lax.axis_index("leaf")
    partners = [me + 2**l * (1 - 2 * ((me // 2**l) % 2)) for l in range(levels)]

    barrier = pltpu.get_barrier_semaphore()
    for partner in partners:
        pl.semaphore_signal(barrier, inc=1, device_id=(partner,), device_id_type=pl.DeviceIdType.MESH)
    pl.semaphore_wait(barrier, levels)

    used = 0
    copies = [[] for _ in range(levels)]

    def send(level, rows, columns):
        nonlocal used
        copy = pltpu.make_async_remote_copy(
            src_ref=mine[level].at[rows, columns],
            dst_ref=theirs[level].at[rows, columns],
            send_sem=send_sem.at[used],
            recv_sem=recv_sem.at[used],
            device_id=(partners[level],),
            device_id_type=pl.DeviceIdType.MESH,
        )
        used += 1
        copy.start()
        copies[level].append(copy)

    def send_row(level, m):
        end = (levels - level + 1) * R
        rows = slice(m * R, (m + 1) * R)
        if m == 0:
            send(level, rows, slice(0, R))
            send(level, rows, slice(R, end))
        else:
            send(level, rows, slice(m * R, end))

    for m in range(levels):
        send_row(0, m)
    eye = (
        lax.broadcasted_iota(jnp.int32, (R, R), 0) == lax.broadcasted_iota(jnp.int32, (R, R), 1)
    ).astype(F32)
    for level in range(levels):
        left = levels - level
        end = (left + 1) * R
        copies[level][0].wait_recv()
        work[...] = eye + (mine[level][0:R, 0:R] + theirs[level][0:R, 0:R])
        negative_inverse(work)
        copies[level][1].wait_recv()
        rest = mine[level][0:R, R:end] + theirs[level][0:R, R:end]
        theirs[level][0:R, R:end] = rest
        weights[level][...] = product(-work[...], rest)
        for m in range(1, left):
            copies[level][m + 1].wait_recv()
            rows = slice(m * R, (m + 1) * R)
            mine[level + 1][(m - 1) * R : m * R, (m - 1) * R : end - R] = (
                mine[level][rows, m * R : end] + theirs[level][rows, m * R : end]
            ) - product(theirs[level][0:R, rows], weights[level][:, (m - 1) * R : end - R], 0)
            send_row(level + 1, m - 1)
    for level in reversed(range(levels)):
        left = levels - level
        part = weights[level][:, (left - 1) * R :]
        if level < levels - 1:
            part = part - product(weights[level][:, : (left - 1) * R], coefficients[(level + 1) * R :, :])
        coefficients[level * R : (level + 1) * R, :] = part
    for level in range(levels):
        for copy in copies[level]:
            copy.wait_send()


def tree(gram):
    levels = gram.shape[0] // R
    shapes = [((levels - l) * R, (levels - l + 1) * R) for l in range(levels)]
    count = sum(levels - l + 1 for l in range(levels))
    vmem = pl.BlockSpec(memory_space=pltpu.VMEM)
    return pl.pallas_call(
        functools.partial(tree_kernel, levels),
        out_shape=jax.ShapeDtypeStruct((levels * R, R), F32),
        in_specs=[vmem],
        out_specs=vmem,
        scratch_shapes=[pltpu.VMEM(s, F32) for s in shapes[1:]]
        + [pltpu.VMEM(s, F32) for s in shapes]
        + [pltpu.VMEM((R, s[0]), F32) for s in shapes]
        + [
            pltpu.VMEM((R, R), F32),
            pltpu.SemaphoreType.DMA((count,)),
            pltpu.SemaphoreType.DMA((count,)),
        ],
        compiler_params=pltpu.CompilerParams(
            collective_id=0, has_side_effects=True, vmem_limit_bytes=56 * 2**20
        ),
    )(gram)


def body(white_noise, leaf_inverse, bases):
    split = bases.shape[1]
    right_side = jnp.concatenate([bases, white_noise], axis=1)
    solved = jnp.dot(leaf_inverse, right_side, precision=lax.Precision.HIGH, preferred_element_type=F32)
    gram = lax.dot_general(
        bases, solved, (((0,), (0,)), ((), ())), precision=lax.Precision.HIGH, preferred_element_type=F32
    )
    coefficients = tree(gram)
    return solved[:, split:] - jnp.dot(
        solved[:, :split], coefficients, precision=lax.Precision.HIGH, preferred_element_type=F32
    )


def solution(mesh):
    in_specs = (P("leaf", None), P("leaf", None), P("leaf", None))
    out_specs = P("leaf", None)
    return jax.shard_map(body, mesh=mesh, in_specs=in_specs, out_specs=out_specs, check_vma=False)
```

```python
import functools

import jax
import jax.numpy as jnp
from jax import lax
from jax.experimental import pallas as pl
from jax.experimental.pallas import tpu as pltpu
from jax.sharding import PartitionSpec as P

R = 128
PANEL = 16
F32 = jnp.float32
BF16 = jnp.bfloat16


def split2(x):
    high = x.astype(BF16)
    return high, (x - high.astype(F32)).astype(BF16)


def split3(x):
    high = x.astype(BF16)
    rest = x - high.astype(F32)
    mid = rest.astype(BF16)
    return high, mid, (rest - mid.astype(F32)).astype(BF16)


def mxu(a, b, dim):
    return lax.dot_general(a, b, (((dim,), (0,)), ((), ())), preferred_element_type=F32)


def product(a, b, dim=1):
    a_high, a_low = split2(a)
    b_high, b_low = split2(b)
    return mxu(a_high, b_high, dim) + (mxu(a_high, b_low, dim) + mxu(a_low, b_high, dim))


def negative_inverse(work, between):
    size = work.shape[0]
    row = lax.broadcasted_iota(jnp.int32, (PANEL, size), 0)
    lane = lax.broadcasted_iota(jnp.int32, (PANEL, size), 1)
    whole_row = lax.broadcasted_iota(jnp.int32, (size, size), 0)
    whole_lane = lax.broadcasted_iota(jnp.int32, (size, size), 1)

    def step(block, carry):
        base = pl.multiple_of(block * PANEL, PANEL)
        panel = work[pl.ds(base, PANEL), :]
        columns = [
            jnp.broadcast_to(
                jnp.sum(jnp.where(lane == base + j, panel, 0.0), axis=1, keepdims=True), (PANEL, size)
            )
            for j in range(PANEL)
        ]
        inside = (lane >= base) & (lane < base + PANEL)
        bordered = jnp.where(inside, jnp.where(lane == base + row, -1.0, 0.0), panel)
        reduced = bordered
        scale = jnp.ones((PANEL, size), F32)
        for k in range(PANEL):
            pivot = 1.0 / jnp.broadcast_to(columns[k][k : k + 1], (PANEL, size))
            factor = jnp.where(row == k, 0.0, columns[k] * pivot)
            scale = jnp.where(row == k, pivot, scale)
            for j in range(k + 1, PANEL):
                columns[j] = columns[j] - factor * jnp.broadcast_to(columns[j][k : k + 1], (PANEL, size))
            reduced = reduced - factor * jnp.broadcast_to(reduced[k : k + 1], (PANEL, size))
        a1, a2, a3 = split3(bordered)
        b1, b2, b3 = split3(reduced * scale)
        update = mxu(
            jnp.concatenate([a1, a1, a2, a1, a3, a2], axis=0),
            jnp.concatenate([b1, b2, b1, b3, b1, b2], axis=0),
            0,
        )
        crossed = (whole_row >= base) & (whole_row < base + PANEL)
        crossed |= (whole_lane >= base) & (whole_lane < base + PANEL)
        work[...] = jnp.where(crossed, 0.0, work[...]) - update
        return carry

    steps = size // PANEL
    early = steps * 3 // 4
    lax.fori_loop(0, early, step, 0)
    between()
    lax.fori_loop(early, steps, step, 0)


def tree_kernel(levels, gram, coefficients, *scratch):
    mine = [gram] + list(scratch[: levels - 1])
    theirs = scratch[levels - 1 : 2 * levels - 1]
    weights = scratch[2 * levels - 1 : 3 * levels - 1]
    rest, work, send_sem, recv_sem = scratch[3 * levels - 1 :]
    me = lax.axis_index("leaf")
    partners = [me + 2**l * (1 - 2 * ((me // 2**l) % 2)) for l in range(levels)]
    half = R // 2
    offset = (me % 2) * half

    barrier = pltpu.get_barrier_semaphore()
    for partner in partners:
        pl.semaphore_signal(barrier, inc=1, device_id=(partner,), device_id_type=pl.DeviceIdType.MESH)
    pl.semaphore_wait(barrier, levels)

    started = []
    direct, passed = {}, {}

    def start(source, target, partner):
        copy = pltpu.make_async_remote_copy(
            src_ref=source,
            dst_ref=target,
            send_sem=send_sem.at[len(started)],
            recv_sem=recv_sem.at[len(started)],
            device_id=(partner,),
            device_id_type=pl.DeviceIdType.MESH,
        )
        copy.start()
        started.append(copy)
        return copy

    def part(level, m):
        columns = slice(max(m, 1) * R, (levels - level + 1) * R)
        if level == 0:
            return slice(m * R, (m + 1) * R), columns
        return pl.ds(pl.multiple_of(m * R + offset, half), half), columns

    def send_row(level, m):
        if m == 0:
            corner = (slice(0, R), slice(0, R))
            direct[level, -1] = start(mine[level].at[corner], theirs[level].at[corner], partners[level])
        where = part(level, m)
        direct[level, m] = start(mine[level].at[where], theirs[level].at[where], partners[level])

    def pass_on(level, m):
        direct[level, m].wait_recv()
        if level > 0:
            where = part(level, m)
            passed[level, m] = start(theirs[level].at[where], theirs[level].at[where], partners[0])

    def arrived(level, m):
        if level > 0:
            passed[level, m].wait_recv()

    for m in range(levels):
        send_row(0, m)
    eye = (
        lax.broadcasted_iota(jnp.int32, (R, R), 0) == lax.broadcasted_iota(jnp.int32, (R, R), 1)
    ).astype(F32)
    for level in range(levels):
        left = levels - level
        end = (left + 1) * R

        def update(m):
            arrived(level, m)
            rows = slice(m * R, (m + 1) * R)
            mine[level + 1][(m - 1) * R : m * R, (m - 1) * R : end - R] = (
                mine[level][rows, m * R : end] + theirs[level][rows, m * R : end]
            ) - product(rest[:, (m - 1) * R : m * R], weights[level][:, (m - 1) * R : end - R], 0)
            send_row(level + 1, m - 1)

        direct[level, -1].wait_recv()
        work[...] = eye + (mine[level][0:R, 0:R] + theirs[level][0:R, 0:R])
        negative_inverse(work, functools.partial(pass_on, level, 0))
        if left > 1:
            pass_on(level, 1)
        arrived(level, 0)
        rest[:, : end - R] = mine[level][0:R, R:end] + theirs[level][0:R, R:end]
        weights[level][...] = product(-work[...], rest[:, : end - R])
        if left > 1:
            update(1)
        for m in range(2, left):
            pass_on(level, m)
        for m in range(2, left):
            update(m)
    for level in reversed(range(levels)):
        left = levels - level
        column = weights[level][:, (left - 1) * R :]
        if level < levels - 1:
            column = column - product(weights[level][:, : (left - 1) * R], coefficients[(level + 1) * R :, :])
        coefficients[level * R : (level + 1) * R, :] = column
    for copy in started:
        copy.wait_send()


def tree(gram):
    levels = gram.shape[0] // R
    shapes = [((levels - l) * R, (levels - l + 1) * R) for l in range(levels)]
    count = sum((levels - l) * (2 if l else 1) + 1 for l in range(levels))
    vmem = pl.BlockSpec(memory_space=pltpu.VMEM)
    return pl.pallas_call(
        functools.partial(tree_kernel, levels),
        out_shape=jax.ShapeDtypeStruct((levels * R, R), F32),
        in_specs=[vmem],
        out_specs=vmem,
        scratch_shapes=[pltpu.VMEM(s, F32) for s in shapes[1:]]
        + [pltpu.VMEM(s, F32) for s in shapes]
        + [pltpu.VMEM((R, s[0]), F32) for s in shapes]
        + [
            pltpu.VMEM((R, levels * R), F32),
            pltpu.VMEM((R, R), F32),
            pltpu.SemaphoreType.DMA((count,)),
            pltpu.SemaphoreType.DMA((count,)),
        ],
        compiler_params=pltpu.CompilerParams(
            collective_id=0, has_side_effects=True, vmem_limit_bytes=56 * 2**20
        ),
    )(gram)


def leaf_kernel(inverse, bases, noise, solved, gram, high, low):
    tile = inverse.shape[0]
    split = bases.shape[1]
    levels = split // R
    step = pl.program_id(0)

    @pl.when(step == 0)
    def _():
        for ref, columns in ((bases, slice(0, split)), (noise, slice(split, split + noise.shape[1]))):
            high[:, columns], low[:, columns] = split2(ref[...])
        gram[...] = jnp.zeros_like(gram)

    a_high, a_low = split2(inverse[...])
    found = mxu(a_high, high[...], 1) + (mxu(a_high, low[...], 1) + mxu(a_low, high[...], 1))
    solved[...] = found
    s_high, s_low = split2(found)
    rows = pl.ds(pl.multiple_of(step * tile, tile), tile)
    for m in range(levels):
        b_high = high[rows, m * R : (m + 1) * R]
        b_low = low[rows, m * R : (m + 1) * R]
        c_high, c_low = s_high[:, m * R :], s_low[:, m * R :]
        gram[m * R : (m + 1) * R, m * R :] += mxu(b_high, c_high, 0) + (
            mxu(b_high, c_low, 0) + mxu(b_low, c_high, 0)
        )


def leaf(leaf_inverse, bases, noise):
    cells, split = bases.shape
    width = split + noise.shape[1]
    tile = min(cells, 256)
    whole = lambda i: (0, 0)
    return pl.pallas_call(
        leaf_kernel,
        grid=(cells // tile,),
        out_shape=(
            jax.ShapeDtypeStruct((cells, width), F32),
            jax.ShapeDtypeStruct((split, width), F32),
        ),
        in_specs=[
            pl.BlockSpec((tile, cells), lambda i: (i, 0)),
            pl.BlockSpec(bases.shape, whole),
            pl.BlockSpec(noise.shape, whole),
        ],
        out_specs=(pl.BlockSpec((tile, width), lambda i: (i, 0)), pl.BlockSpec((split, width), whole)),
        scratch_shapes=[pltpu.VMEM((cells, width), BF16), pltpu.VMEM((cells, width), BF16)],
        compiler_params=pltpu.CompilerParams(vmem_limit_bytes=56 * 2**20),
    )(leaf_inverse, bases, noise)


def body(white_noise, leaf_inverse, bases):
    split = bases.shape[1]
    solved, gram = leaf(leaf_inverse, bases, white_noise)
    coefficients = tree(gram)
    return solved[:, split:] - jnp.dot(
        solved[:, :split], coefficients, precision=lax.Precision.HIGH, preferred_element_type=F32
    )


def solution(mesh):
    in_specs = (P("leaf", None), P("leaf", None), P("leaf", None))
    out_specs = P("leaf", None)
    return jax.shard_map(body, mesh=mesh, in_specs=in_specs, out_specs=out_specs, check_vma=False)
```

```python
import functools

import jax
import jax.numpy as jnp
from jax import lax
from jax.experimental import pallas as pl
from jax.experimental.pallas import tpu as pltpu
from jax.sharding import PartitionSpec as P

R = 128
PANEL = 16
F32 = jnp.float32
BF16 = jnp.bfloat16


def split2(x):
    high = x.astype(BF16)
    return high, (x - high.astype(F32)).astype(BF16)


def split3(x):
    high = x.astype(BF16)
    rest = x - high.astype(F32)
    mid = rest.astype(BF16)
    return high, mid, (rest - mid.astype(F32)).astype(BF16)


def mxu(a, b, dim):
    return lax.dot_general(a, b, (((dim,), (0,)), ((), ())), preferred_element_type=F32)


def product(a, b, dim=1):
    a_high, a_low = split2(a)
    b_high, b_low = split2(b)
    return mxu(a_high, b_high, dim) + (mxu(a_high, b_low, dim) + mxu(a_low, b_high, dim))


def negative_inverse(work, between):
    size = work.shape[0]
    row = lax.broadcasted_iota(jnp.int32, (PANEL, size), 0)
    lane = lax.broadcasted_iota(jnp.int32, (PANEL, size), 1)
    whole_row = lax.broadcasted_iota(jnp.int32, (size, size), 0)
    whole_lane = lax.broadcasted_iota(jnp.int32, (size, size), 1)

    def step(block, carry):
        base = pl.multiple_of(block * PANEL, PANEL)
        panel = work[pl.ds(base, PANEL), :]
        columns = [
            jnp.broadcast_to(
                jnp.sum(jnp.where(lane == base + j, panel, 0.0), axis=1, keepdims=True), (PANEL, size)
            )
            for j in range(PANEL)
        ]
        inside = (lane >= base) & (lane < base + PANEL)
        bordered = jnp.where(inside, jnp.where(lane == base + row, -1.0, 0.0), panel)
        reduced = bordered
        scale = jnp.ones((PANEL, size), F32)
        for k in range(PANEL):
            pivot = 1.0 / jnp.broadcast_to(columns[k][k : k + 1], (PANEL, size))
            factor = jnp.where(row == k, 0.0, columns[k] * pivot)
            scale = jnp.where(row == k, pivot, scale)
            for j in range(k + 1, PANEL):
                columns[j] = columns[j] - factor * jnp.broadcast_to(columns[j][k : k + 1], (PANEL, size))
            reduced = reduced - factor * jnp.broadcast_to(reduced[k : k + 1], (PANEL, size))
        a1, a2, a3 = split3(bordered)
        b1, b2, b3 = split3(reduced * scale)
        update = mxu(
            jnp.concatenate([a1, a1, a2, a1, a3, a2], axis=0),
            jnp.concatenate([b1, b2, b1, b3, b1, b2], axis=0),
            0,
        )
        crossed = (whole_row >= base) & (whole_row < base + PANEL)
        crossed |= (whole_lane >= base) & (whole_lane < base + PANEL)
        work[...] = jnp.where(crossed, 0.0, work[...]) - update
        return carry

    steps = size // PANEL
    early = steps * 3 // 4
    lax.fori_loop(0, early, step, 0)
    between()
    lax.fori_loop(early, steps, step, 0)


def leaf_products(inverse, bases, noise, turned_high, turned_low, high, low, noise_solved, gram):
    cells, split = bases.shape
    width = split + noise.shape[1]
    for start in range(0, width, 2 * R):
        stop = min(start + 2 * R, width)
        pieces = [bases[:, start : min(stop, split)]] if start < split else []
        if stop > split:
            pieces.append(noise[:, max(start, split) - split : stop - split])
        r_high, r_low = split2(jnp.concatenate(pieces, axis=1))
        a_high, a_low = split2(inverse[...])
        found = mxu(a_high, r_high, 1) + (mxu(a_high, r_low, 1) + mxu(a_low, r_high, 1))
        inner = min(stop, split)
        if start < split:
            fresh = slice(start, inner)
            turned_high[fresh, :], turned_low[fresh, :] = split2(bases[:, fresh].T)
        s_high, s_low = split2(found)
        if start < split:
            high[:, fresh], low[:, fresh] = s_high[:, : inner - start], s_low[:, : inner - start]
        if stop > split:
            noise_solved[:, max(start, split) - split : stop - split] = found[:, max(start, split) - start :]
        b_high = turned_high[:inner, :]
        gram[:inner, start:stop] = mxu(b_high, s_high, 1) + (
            mxu(b_high, s_low, 1) + mxu(turned_low[:inner, :], s_high, 1)
        )


def tree_kernel(levels, noise, inverse, bases, solution_ref, *scratch):
    mine = scratch[:levels]
    theirs = scratch[levels : 2 * levels]
    high, low, turned_high, turned_low, weights, rest, work, send_sem, recv_sem = scratch[2 * levels :]
    split = levels * R
    me = lax.axis_index("leaf")
    partners = [me + 2**l * (1 - 2 * ((me // 2**l) % 2)) for l in range(levels)]
    half = R // 2
    offset = (me % 2) * half

    barrier = pltpu.get_barrier_semaphore()
    for partner in partners:
        pl.semaphore_signal(barrier, inc=1, device_id=(partner,), device_id_type=pl.DeviceIdType.MESH)
    leaf_products(inverse, bases, noise, turned_high, turned_low, high, low, solution_ref, mine[0])
    pl.semaphore_wait(barrier, levels)

    started = []
    direct, passed = {}, {}

    def start(source, target, partner):
        copy = pltpu.make_async_remote_copy(
            src_ref=source,
            dst_ref=target,
            send_sem=send_sem.at[len(started)],
            recv_sem=recv_sem.at[len(started)],
            device_id=(partner,),
            device_id_type=pl.DeviceIdType.MESH,
        )
        copy.start()
        started.append(copy)
        return copy

    def part(level, m):
        columns = slice(max(m, 1) * R, (levels - level + 1) * R)
        if level == 0:
            return slice(m * R, (m + 1) * R), columns
        return pl.ds(pl.multiple_of(m * R + offset, half), half), columns

    def send_row(level, m):
        if m == 0:
            corner = (slice(0, R), slice(0, R))
            direct[level, -1] = start(mine[level].at[corner], theirs[level].at[corner], partners[level])
        where = part(level, m)
        direct[level, m] = start(mine[level].at[where], theirs[level].at[where], partners[level])

    def pass_on(level, m):
        direct[level, m].wait_recv()
        if level > 0:
            where = part(level, m)
            passed[level, m] = start(theirs[level].at[where], theirs[level].at[where], partners[0])

    def arrived(level, m):
        if level > 0:
            passed[level, m].wait_recv()

    for m in range(levels):
        send_row(0, m)
    eye = (
        lax.broadcasted_iota(jnp.int32, (R, R), 0) == lax.broadcasted_iota(jnp.int32, (R, R), 1)
    ).astype(F32)
    for level in range(levels):
        left = levels - level
        end = (left + 1) * R
        here = slice(level * R, (level + 1) * R)
        later = (level + 1) * R

        def update(m):
            arrived(level, m)
            rows = slice(m * R, (m + 1) * R)
            mine[level + 1][(m - 1) * R : m * R, (m - 1) * R : end - R] = (
                mine[level][rows, m * R : end] + theirs[level][rows, m * R : end]
            ) - product(rest[:, (m - 1) * R : m * R], weights[here, (level + m) * R :], 0)
            send_row(level + 1, m - 1)

        direct[level, -1].wait_recv()
        work[...] = eye + (mine[level][0:R, 0:R] + theirs[level][0:R, 0:R])
        negative_inverse(work, functools.partial(pass_on, level, 0))
        if left > 1:
            pass_on(level, 1)
        arrived(level, 0)
        rest[:, : end - R] = mine[level][0:R, R:end] + theirs[level][0:R, R:end]
        weights[here, later:] = product(-work[...], rest[:, : end - R])
        if left > 1:
            update(1)
        for m in range(2, left):
            pass_on(level, m)
        for m in range(2, left):
            update(m)
        if level > 0:
            above = slice(0, level * R)
            weights[above, later:] = weights[above, later:] - product(
                weights[above, here], weights[here, later:]
            )
    w_high, w_low = split2(weights[:, split:])
    solution_ref[...] = solution_ref[...] - (
        mxu(high[...], w_high, 1) + (mxu(high[...], w_low, 1) + mxu(low[...], w_high, 1))
    )
    for copy in started:
        copy.wait_send()


def body(white_noise, leaf_inverse, bases):
    cells, split = bases.shape
    levels = split // R
    shapes = [((levels - l) * R, (levels - l + 1) * R) for l in range(levels)]
    count = sum((levels - l) * (2 if l else 1) + 1 for l in range(levels))
    vmem = pl.BlockSpec(memory_space=pltpu.VMEM)
    return pl.pallas_call(
        functools.partial(tree_kernel, levels),
        out_shape=jax.ShapeDtypeStruct(white_noise.shape, F32),
        in_specs=[vmem] * 3,
        out_specs=vmem,
        scratch_shapes=[pltpu.VMEM(s, F32) for s in shapes + shapes]
        + [
            pltpu.VMEM((cells, split), BF16),
            pltpu.VMEM((cells, split), BF16),
            pltpu.VMEM((split, cells), BF16),
            pltpu.VMEM((split, cells), BF16),
            pltpu.VMEM(shapes[0], F32),
            pltpu.VMEM((R, split), F32),
            pltpu.VMEM((R, R), F32),
            pltpu.SemaphoreType.DMA((count,)),
            pltpu.SemaphoreType.DMA((count,)),
        ],
        compiler_params=pltpu.CompilerParams(
            collective_id=0, has_side_effects=True, vmem_limit_bytes=60 * 2**20
        ),
    )(white_noise, leaf_inverse, bases)


def solution(mesh):
    in_specs = (P("leaf", None), P("leaf", None), P("leaf", None))
    out_specs = P("leaf", None)
    return jax.shard_map(body, mesh=mesh, in_specs=in_specs, out_specs=out_specs, check_vma=False)
```

```python
import functools

import jax
import jax.numpy as jnp
from jax import lax
from jax.experimental import pallas as pl
from jax.experimental.pallas import tpu as pltpu
from jax.sharding import PartitionSpec as P

R = 128
PANEL = 16
F32 = jnp.float32
BF16 = jnp.bfloat16


def split2(x):
    high = x.astype(BF16)
    return high, (x - high.astype(F32)).astype(BF16)


def split3(x):
    high = x.astype(BF16)
    rest = x - high.astype(F32)
    mid = rest.astype(BF16)
    return high, mid, (rest - mid.astype(F32)).astype(BF16)


def mxu(a, b, dim):
    return lax.dot_general(a, b, (((dim,), (0,)), ((), ())), preferred_element_type=F32)


def product(a, b, dim=1):
    a_high, a_low = split2(a)
    b_high, b_low = split2(b)
    return mxu(a_high, b_high, dim) + (mxu(a_high, b_low, dim) + mxu(a_low, b_high, dim))


def negative_inverse(work, between):
    size = work.shape[0]
    row = lax.broadcasted_iota(jnp.int32, (PANEL, size), 0)
    lane = lax.broadcasted_iota(jnp.int32, (PANEL, size), 1)
    whole_row = lax.broadcasted_iota(jnp.int32, (size, size), 0)
    whole_lane = lax.broadcasted_iota(jnp.int32, (size, size), 1)

    def step(block, carry):
        base = pl.multiple_of(block * PANEL, PANEL)
        panel = work[pl.ds(base, PANEL), :]
        columns = [
            jnp.broadcast_to(
                jnp.sum(jnp.where(lane == base + j, panel, 0.0), axis=1, keepdims=True), (PANEL, size)
            )
            for j in range(PANEL)
        ]
        inside = (lane >= base) & (lane < base + PANEL)
        bordered = jnp.where(inside, jnp.where(lane == base + row, -1.0, 0.0), panel)
        reduced = bordered
        scale = jnp.ones((PANEL, size), F32)
        for k in range(PANEL):
            pivot = 1.0 / jnp.broadcast_to(columns[k][k : k + 1], (PANEL, size))
            factor = jnp.where(row == k, 0.0, columns[k] * pivot)
            scale = jnp.where(row == k, pivot, scale)
            for j in range(k + 1, PANEL):
                columns[j] = columns[j] - factor * jnp.broadcast_to(columns[j][k : k + 1], (PANEL, size))
            reduced = reduced - factor * jnp.broadcast_to(reduced[k : k + 1], (PANEL, size))
        a1, a2, a3 = split3(bordered)
        b1, b2, b3 = split3(reduced * scale)
        update = mxu(
            jnp.concatenate([a1, a1, a2, a1, a3, a2], axis=0),
            jnp.concatenate([b1, b2, b1, b3, b1, b2], axis=0),
            0,
        )
        crossed = (whole_row >= base) & (whole_row < base + PANEL)
        crossed |= (whole_lane >= base) & (whole_lane < base + PANEL)
        work[...] = jnp.where(crossed, 0.0, work[...]) - update
        return carry

    steps = size // PANEL
    early = steps * 3 // 4
    lax.fori_loop(0, early, step, 0)
    between()
    lax.fori_loop(early, steps, step, 0)


def leaf_products(inverse, bases, noise, turned_high, turned_low, high, low, noise_solved, gram, corner_done):
    cells, split = bases.shape
    width = split + noise.shape[1]
    for start in range(0, width, 2 * R):
        stop = min(start + 2 * R, width)
        pieces = [bases[:, start : min(stop, split)]] if start < split else []
        if stop > split:
            pieces.append(noise[:, max(start, split) - split : stop - split])
        r_high, r_low = split2(jnp.concatenate(pieces, axis=1))
        a_high, a_low = split2(inverse[...])
        found = mxu(a_high, r_high, 1) + (mxu(a_high, r_low, 1) + mxu(a_low, r_high, 1))
        inner = min(stop, split)
        if start < split:
            fresh = slice(start, inner)
            turned_high[fresh, :], turned_low[fresh, :] = split2(bases[:, fresh].T)
        s_high, s_low = split2(found)
        if start < split:
            high[:, fresh], low[:, fresh] = s_high[:, : inner - start], s_low[:, : inner - start]
        if stop > split:
            noise_solved[:, max(start, split) - split : stop - split] = found[:, max(start, split) - start :]
        b_high = turned_high[:inner, :]
        gram[:inner, start:stop] = mxu(b_high, s_high, 1) + (
            mxu(b_high, s_low, 1) + mxu(turned_low[:inner, :], s_high, 1)
        )
        if start == 0:
            corner_done()


def tree_kernel(levels, noise, inverse, bases, solution_ref, *scratch):
    mine = scratch[:levels]
    theirs = scratch[levels : 2 * levels]
    high, low, turned_high, turned_low, weights, rest, work, send_sem, recv_sem = scratch[2 * levels :]
    split = levels * R
    me = lax.axis_index("leaf")
    partners = [me + 2**l * (1 - 2 * ((me // 2**l) % 2)) for l in range(levels)]
    half = R // 2
    offset = (me % 2) * half

    barrier = pltpu.get_barrier_semaphore()
    for partner in partners:
        pl.semaphore_signal(barrier, inc=1, device_id=(partner,), device_id_type=pl.DeviceIdType.MESH)
    started = []
    direct, passed = {}, {}

    def start(source, target, partner):
        copy = pltpu.make_async_remote_copy(
            src_ref=source,
            dst_ref=target,
            send_sem=send_sem.at[len(started)],
            recv_sem=recv_sem.at[len(started)],
            device_id=(partner,),
            device_id_type=pl.DeviceIdType.MESH,
        )
        copy.start()
        started.append(copy)
        return copy

    def part(level, m):
        columns = slice(max(m, 1) * R, (levels - level + 1) * R)
        if level == 0:
            return slice(m * R, (m + 1) * R), columns
        return pl.ds(pl.multiple_of(m * R + offset, half), half), columns

    def send_corner(level):
        corner = (slice(0, R), slice(0, R))
        direct[level, -1] = start(mine[level].at[corner], theirs[level].at[corner], partners[level])

    def send_row(level, m):
        where = part(level, m)
        direct[level, m] = start(mine[level].at[where], theirs[level].at[where], partners[level])

    def pass_on(level, m):
        direct[level, m].wait_recv()
        if level > 0:
            where = part(level, m)
            passed[level, m] = start(theirs[level].at[where], theirs[level].at[where], partners[0])

    def arrived(level, m):
        if level > 0:
            passed[level, m].wait_recv()

    def corner_done():
        pl.semaphore_wait(barrier, levels)
        send_corner(0)

    leaf_products(
        inverse, bases, noise, turned_high, turned_low, high, low, solution_ref, mine[0], corner_done
    )
    for m in range(levels):
        send_row(0, m)
    eye = (
        lax.broadcasted_iota(jnp.int32, (R, R), 0) == lax.broadcasted_iota(jnp.int32, (R, R), 1)
    ).astype(F32)
    for level in range(levels):
        left = levels - level
        end = (left + 1) * R
        here = slice(level * R, (level + 1) * R)
        later = (level + 1) * R

        def update(m):
            arrived(level, m)
            rows = slice(m * R, (m + 1) * R)
            mine[level + 1][(m - 1) * R : m * R, (m - 1) * R : end - R] = (
                mine[level][rows, m * R : end] + theirs[level][rows, m * R : end]
            ) - product(rest[:, (m - 1) * R : m * R], weights[here, (level + m) * R :], 0)
            if m == 1:
                send_corner(level + 1)
            send_row(level + 1, m - 1)

        direct[level, -1].wait_recv()
        work[...] = eye + (mine[level][0:R, 0:R] + theirs[level][0:R, 0:R])
        negative_inverse(work, functools.partial(pass_on, level, 0))
        if left > 1:
            pass_on(level, 1)
        arrived(level, 0)
        rest[:, : end - R] = mine[level][0:R, R:end] + theirs[level][0:R, R:end]
        weights[here, later:] = product(-work[...], rest[:, : end - R])
        if left > 1:
            update(1)
        for m in range(2, left):
            pass_on(level, m)
        for m in range(2, left):
            update(m)
        if level > 0:
            above = slice(0, level * R)
            weights[above, later:] = weights[above, later:] - product(
                weights[above, here], weights[here, later:]
            )
    w_high, w_low = split2(weights[:, split:])
    solution_ref[...] = solution_ref[...] - (
        mxu(high[...], w_high, 1) + (mxu(high[...], w_low, 1) + mxu(low[...], w_high, 1))
    )
    for copy in started:
        copy.wait_send()


def body(white_noise, leaf_inverse, bases):
    cells, split = bases.shape
    levels = split // R
    shapes = [((levels - l) * R, (levels - l + 1) * R) for l in range(levels)]
    count = sum((levels - l) * (2 if l else 1) + 1 for l in range(levels))
    vmem = pl.BlockSpec(memory_space=pltpu.VMEM)
    return pl.pallas_call(
        functools.partial(tree_kernel, levels),
        out_shape=jax.ShapeDtypeStruct(white_noise.shape, F32),
        in_specs=[vmem] * 3,
        out_specs=vmem,
        scratch_shapes=[pltpu.VMEM(s, F32) for s in shapes + shapes]
        + [
            pltpu.VMEM((cells, split), BF16),
            pltpu.VMEM((cells, split), BF16),
            pltpu.VMEM((split, cells), BF16),
            pltpu.VMEM((split, cells), BF16),
            pltpu.VMEM(shapes[0], F32),
            pltpu.VMEM((R, split), F32),
            pltpu.VMEM((R, R), F32),
            pltpu.SemaphoreType.DMA((count,)),
            pltpu.SemaphoreType.DMA((count,)),
        ],
        compiler_params=pltpu.CompilerParams(
            collective_id=0, has_side_effects=True, vmem_limit_bytes=60 * 2**20
        ),
    )(white_noise, leaf_inverse, bases)


def solution(mesh):
    in_specs = (P("leaf", None), P("leaf", None), P("leaf", None))
    out_specs = P("leaf", None)
    return jax.shard_map(body, mesh=mesh, in_specs=in_specs, out_specs=out_specs, check_vma=False)
```
